256 devices in a mesh: fsdp: 64 (over z, x, y_lo), tp: 4 (over y_hi, core).
Axes of the slice: x: 4, y: 4 (y_hi: 2, y_lo: 2; y = y_hi * 2 + y_lo), z: 8, core: 2. Of those that a mesh axis runs over, the one named last changes fastest.
Arguments:
- grad: bfloat16 [4096, 8192], P('fsdp', 'tp'), may hold values from -6 to 6
- left_codes: bfloat16 [2, 2048, 2048], P(None, 'fsdp', 'tp'), may hold values from -0.125 to 0.125
- left_scale: bfloat16 [2, 2048], P(None, 'fsdp'), may hold values from 0.5 to 2
- right_codes: bfloat16 [4, 2048, 2048], P('tp', 'fsdp'), may hold values from -0.125 to 0.125
- right_scale: bfloat16 [4, 2048], P('tp', 'fsdp'), may hold values from 0.5 to 2
- moment1: float32 [4096, 8192], P('fsdp', 'tp'), may hold values from -3 to 3
- moment2: float32 [4096, 8192], P('fsdp', 'tp'), may hold values from 0.002 to 0.02
Outputs:
- update: float32 [4096, 8192], P('fsdp', 'tp')
- moment1_new: float32 [4096, 8192], P('fsdp', 'tp')
- moment2_new: float32 [4096, 8192], P('fsdp', 'tp')
The draws below stay inside these ranges and needn't reach their ends.
All inputs are finite; a program needn't handle non-finite values.
Results may differ from the reference program's by a relative error of at most 0.00045.
Values may be sent and summed in bfloat16 or wider, within the bound.
No kernel may reach another device: no remote copies, remote signals or barrier semaphores. Data moves between devices by JAX's collectives and lax.ppermute only.
A program may use at most 128 MiB of HBM per device.

```python
import math
import jax
import jax.numpy as jnp
from jax import lax

B = 2048
LBLOCKS = 2
R = 4096
RBLOCKS = 4
C = 8192


def shard_levels(stream_key, extent, split, low, largest):
    gain, own = 1.0, jax.random.fold_in(stream_key, 6)
    for dim, blocks in split:
        steps = jnp.exp(jax.random.uniform(jax.random.fold_in(own, dim), (blocks,), jnp.float32, low / len(split), largest / len(split)))
        gain = gain * jnp.repeat(steps, extent[dim] // blocks).reshape([-1 if axis == dim else 1 for axis in range(len(extent))])
    return gain


def centred(stream_key, shape, deviation, most, cuts=(), dtype=jnp.bfloat16):
    array = deviation * jax.random.normal(stream_key, shape, jnp.float32)
    if cuts:
        array = array * shard_levels(stream_key, shape, cuts, -0.22, 0.18)
    return jnp.clip(array, -most, most).astype(dtype)


def setup_inputs(seed: int = 0) -> dict:
    arg_keys = jax.random.split(jax.random.key(seed), 8)
    grad = centred(arg_keys[0], (R, C), 1.0, 6.0, ((0, 64), (1, 4)))
    left_codes = centred(arg_keys[1], (LBLOCKS, B, B), B ** -0.5, 0.125, ((1, 64), (2, 4)))
    left_scale = jnp.clip(jnp.exp(math.log(2.0) - 1.3862944 * jax.random.uniform(arg_keys[2], (LBLOCKS, B), jnp.float32) ** shard_levels(arg_keys[2], (LBLOCKS, B), ((1, 64),), -0.2, 0.2)), 0.5, 2.0).astype(jnp.bfloat16)
    right_codes = centred(arg_keys[3], (RBLOCKS, B, B), B ** -0.5, 0.125, ((0, 4), (1, 64)))
    right_scale = jnp.clip(jnp.exp(math.log(2.0) - 1.3862944 * jax.random.uniform(arg_keys[4], (RBLOCKS, B), jnp.float32) ** shard_levels(arg_keys[4], (RBLOCKS, B), ((0, 4), (1, 64)), -0.2, 0.2)), 0.5, 2.0).astype(jnp.bfloat16)
    moment1 = centred(arg_keys[5], (R, C), 0.5, 3.0, ((0, 64), (1, 4)), jnp.float32)
    moment2 = jnp.clip(jnp.exp(math.log(0.02) - 2.30258502 * jax.random.uniform(arg_keys[6], (R, C), jnp.float32) ** shard_levels(arg_keys[6], (R, C), ((0, 64), (1, 4)), -0.2, 0.2)), 0.002, 0.02)
    return dict(grad=grad, left_codes=left_codes, left_scale=left_scale, right_codes=right_codes, right_scale=right_scale, moment1=moment1, moment2=moment2)


beta_one = 0.9
beta_two = 0.999
corr_one = 1.0 - 0.9 ** 10
corr_two = 1.0 - 0.999 ** 10
epsilon = 1e-08

def reference(grad, left_codes, left_scale, right_codes, right_scale, moment1, moment2):
    highest = lax.Precision.HIGHEST
    left_blocks = left_codes.astype(jnp.float32) * left_scale.astype(jnp.float32)[:, :, None]
    right = right_codes.astype(jnp.float32) * right_scale.astype(jnp.float32)[:, :, None]
    gradient = grad.astype(jnp.float32).reshape(LBLOCKS, B, RBLOCKS, B)
    half_rot = jnp.einsum('bio,bitc->botc', left_blocks, gradient, precision=highest)
    rotated = jnp.einsum('botc,tck->botk', half_rot, right, precision=highest).reshape(R, C)
    first_new = beta_one * moment1 + (1.0 - beta_one) * rotated
    second_new = beta_two * moment2 + (1.0 - beta_two) * rotated * rotated
    direction = first_new / corr_one / (jnp.sqrt(second_new / corr_two) + epsilon)
    back_rot = jnp.einsum('botk,tck->botc', direction.reshape(LBLOCKS, B, RBLOCKS, B), right, precision=highest)
    update = jnp.einsum('bio,botc->bitc', left_blocks, back_rot, precision=highest).reshape(R, C)
    return (update, first_new, second_new)
```

```python
import jax
import jax.numpy as jnp
from jax import lax
from jax.sharding import Mesh, PartitionSpec as P

beta_one = 0.9
beta_two = 0.999
corr_one = 1.0 - 0.9**10
corr_two = 1.0 - 0.999**10
epsilon = 1e-08

AXES = ("zh", "zl", "x", "l", "h", "c")
SIZES = (2, 4, 4, 2, 2, 2)
F32, BF16, F16 = jnp.float32, jnp.bfloat16, jnp.float16
WIDTH = 2048
SLICE = 256
PLANE = 512
LANES = 128


def linear(zh, zl, x, l, h, c):
    index = 0
    for size, value in zip(SIZES, (zh, zl, x, l, h, c)):
        index = index * size + value
    return index


def left_perms():
    first, second = [], []
    for z in range(8):
        for x in range(4):
            for l in range(2):
                for t in range(4):
                    src = linear(z // 4, z % 4, x, l, t // 2, t % 2)
                    for perm, b in ((first, l), (second, 1 - l)):
                        perm.append((src, linear(b, t, x, z % 2, z // 2 % 2, z // 4)))
    return first, second


def split(value):
    high = lax.reduce_precision(value, 8, 7)
    return high.astype(BF16), (value - high).astype(BF16)


def exponent(bound):
    return jnp.ceil(jnp.log2(jnp.maximum(bound, 1e-30))) + 1.0


def dot(a, b, dims):
    return lax.dot_general(a, b, ((dims[:1], dims[1:]), ((), ())), preferred_element_type=F32)


def with_lanes(value, lane):
    return jnp.concatenate([value, jnp.broadcast_to(lane, lane.shape[:-1] + (LANES,)).astype(value.dtype)], -1)


def body(grad, left_codes, left_scale, right_codes, right_scale, moment1, moment2):
    zh, zl, l = (lax.axis_index(a) for a in ("zh", "zl", "l"))
    rows = grad.shape[0]
    right = lax.all_gather(with_lanes(right_codes[0], right_scale[0][:, None]), ("zh", "zl"), axis=0, tiled=True)

    pieces = with_lanes(left_codes, left_scale[..., None])
    first, second = left_perms()
    got1 = lax.ppermute(jnp.where(l == 0, pieces[0], pieces[1]), AXES, first)
    got2 = lax.ppermute(jnp.where(l == 0, pieces[1], pieces[0]), AXES, second)

    slices = grad.reshape(rows, 8, 8, 32).transpose(2, 0, 1, 3).reshape(1, 8, rows, SLICE)
    columns = lax.all_to_all(
        jnp.broadcast_to(slices, (4, 8, rows, SLICE)).reshape(32, rows, SLICE), ("zl", "x", "l"), 0, 0, tiled=True
    ).reshape(WIDTH, SLICE)

    chunk = jnp.where(zh == 0, jnp.concatenate([got1, got2]), jnp.concatenate([got2, got1]))
    part = lax.all_to_all(
        jnp.broadcast_to(chunk[None], (16,) + chunk.shape), ("h", "l", "x"), 0, 0, tiled=True
    ).reshape(1, WIDTH // 2, -1)
    left = lax.all_to_all(jnp.concatenate([part, part]), ("c",), 0, 0, tiled=True).reshape(WIDTH, -1)
    left_rows = left[:, PLANE].astype(F32)[:, None]
    left = left[:, :PLANE]

    high, low = split(columns.astype(F32) * left_rows)
    half = dot(left, jnp.concatenate([high, low], 1), (0, 0))
    half = half[:, :SLICE] + half[:, SLICE:]
    right_rows = right[:, WIDTH].astype(F32)[None, :]
    right = right[:, :WIDTH]
    half = half * right_rows
    power = exponent(0.125 * jnp.sum(jnp.abs(half), axis=1, keepdims=True))
    high, low = split(half * jnp.exp2(15.0 - power))
    partial = dot(high, right, (1, 0)) + dot(low, right, (1, 0))
    message = with_lanes(partial.astype(F16), power)
    got = lax.all_to_all(message.reshape(8, rows, -1), ("x", "l"), 0, 0, tiled=True)
    rotated = jnp.sum(got[..., :WIDTH].astype(F32) * jnp.exp2(got[..., WIDTH:WIDTH + 1].astype(F32) - 15.0), axis=0)

    first_new = beta_one * moment1 + (1.0 - beta_one) * rotated
    second_new = beta_two * moment2 + (1.0 - beta_two) * rotated * rotated
    direction = first_new / corr_one / (jnp.sqrt(second_new / corr_two) + epsilon)

    power = exponent(jnp.max(jnp.abs(direction), axis=1, keepdims=True))
    message = with_lanes((direction * jnp.exp2(15.0 - power)).astype(F16), power)
    got = lax.all_to_all(jnp.broadcast_to(message[None], (8,) + message.shape), ("x", "l"), 0, 0, tiled=True)
    got = got.reshape(PLANE, -1)
    power = got[:, WIDTH:WIDTH + 1].astype(F32)
    top = jnp.max(power)
    tops = jnp.where(jnp.arange(4)[:, None] == zl, top, 0.0) * jnp.ones((1, LANES), F32)
    for shift in range(1, 4):
        other = lax.ppermute(jnp.full((8, LANES), top, F32), ("zl",), [(i, (i + shift) % 4) for i in range(4)])
        tops = tops + jnp.where(jnp.arange(4)[:, None] == (zl - shift) % 4, other[:1], 0.0)
    high, low = split(got[:, :WIDTH].astype(F32))
    back = dot(high, right, (1, 1)) + dot(low, right, (1, 1))
    back = back * right_rows * jnp.exp2(power - 15.0 - 1.0 - top)
    high, low = split(back)
    update = dot(left, jnp.concatenate([high, low], 1), (1, 0))
    update = (update[:, :SLICE] + update[:, SLICE:]) * left_rows
    got = lax.all_to_all(update.astype(F16).reshape(32, rows, SLICE), ("zl", "x", "l"), 0, 0, tiled=True)
    scales = jnp.exp2(tops[:, 0] + 1.0)
    update = jnp.sum(got.reshape(4, 8, rows, SLICE).astype(F32) * scales[:, None, None, None], axis=0)
    update = update.reshape(8, rows, 8, 32).transpose(1, 2, 0, 3).reshape(rows, WIDTH)
    return update, first_new, second_new


def solution(mesh):
    fine = Mesh(mesh.devices.reshape(SIZES), AXES)
    fsdp, tp = ("zh", "zl", "x", "l"), ("h", "c")
    return jax.shard_map(
        body,
        mesh=fine,
        in_specs=(P(fsdp, tp), P(None, fsdp, tp), P(None, fsdp), P(tp, fsdp, None), P(tp, fsdp), P(fsdp, tp), P(fsdp, tp)),
        out_specs=(P(fsdp, tp), P(fsdp, tp), P(fsdp, tp)),
        check_vma=False,
    )
```

```python
import jax
import jax.numpy as jnp
from jax import lax
from jax.experimental import pallas as pl
from jax.experimental.pallas import tpu as pltpu
from jax.sharding import Mesh, PartitionSpec as P

beta_one = 0.9
beta_two = 0.999
corr_one = 1.0 - 0.9**10
corr_two = 1.0 - 0.999**10
epsilon = 1e-08

AXES = ("zh", "zl", "x", "l", "h", "c")
SIZES = (2, 4, 4, 2, 2, 2)
F32, BF16, F16 = jnp.float32, jnp.bfloat16, jnp.float16
WIDTH = 2048
SLICE = 256
PLANE = 512
ROWS = 64
LANES = 128
SWAP = [(0, 1), (1, 0)]


def linear(zh, zl, x, l, h, c):
    index = 0
    for size, value in zip(SIZES, (zh, zl, x, l, h, c)):
        index = index * size + value
    return index


def left_perms():
    first, second = [], []
    for z in range(8):
        for x in range(4):
            for l in range(2):
                for t in range(4):
                    src = linear(z // 4, z % 4, x, l, t // 2, t % 2)
                    for perm, b in ((first, l), (second, 1 - l)):
                        perm.append((src, linear(b, t, x, z % 2, z // 2 % 2, z // 4)))
    return first, second


def split(value):
    high = value.astype(BF16)
    return high, (value - high.astype(F32)).astype(BF16)


def exponent(bound):
    return jnp.ceil(jnp.log2(jnp.maximum(bound, 1e-30))) + 1.0


def dot(a, b, dims):
    return lax.dot_general(a, b, ((dims[:1], dims[1:]), ((), ())), preferred_element_type=F32)


def with_lanes(value, lane):
    return jnp.concatenate([value, jnp.broadcast_to(lane, lane.shape[:-1] + (LANES,)).astype(value.dtype)], -1)


def call(kernel, out, scratch=(), smem=0, operands=()):
    specs = [pl.BlockSpec(memory_space=pltpu.SMEM)] * smem
    specs += [pl.BlockSpec(memory_space=pltpu.VMEM)] * (len(operands) - smem)
    return pl.pallas_call(
        kernel,
        out_shape=tuple(jax.ShapeDtypeStruct(shape, F32) for shape in out),
        in_specs=specs,
        out_specs=tuple(pl.BlockSpec(memory_space=pltpu.VMEM) for _ in out),
        scratch_shapes=list(scratch),
        compiler_params=pltpu.CompilerParams(vmem_limit_bytes=28 * 1024 * 1024),
    )(*operands)


def block_starts(place):
    c, y, x = place[0], place[1], place[2]
    for part in range(2):
        core = c if part == 0 else 1 - c
        for s in range(4):
            for t in range(4):
                block = core * 16 + lax.rem(y - s + 4, 4) * 4 + lax.rem(x - t + 4, 4)
                yield part, (s * 4 + t) * ROWS, pl.multiple_of(block * ROWS, ROWS)


def left_kernel(place, own, other, columns, mine, theirs, scaled, total):
    tiles = (own, other)
    for part, row, start in block_starts(place):
        scale = tiles[part][row:row + ROWS, PLANE:].astype(F32)
        here = part * 1024 + row
        for lane in range(0, SLICE, LANES):
            value = columns[pl.ds(start, ROWS), lane:lane + LANES].astype(F32) * scale
            high, low = split(value)
            scaled[here:here + ROWS, lane:lane + LANES] = high
            scaled[here:here + ROWS, SLICE + lane:SLICE + lane + LANES] = low
    half = dot(own[:, :PLANE], scaled[:1024], (0, 0)) + dot(other[:, :PLANE], scaled[1024:], (0, 0))
    total[...] = half[:, :SLICE] + half[:, SLICE:]
    l = lax.rem(place[1], 2)
    for x in range(4):
        mine[x * ROWS:(x + 1) * ROWS, :] = total[pl.ds(pl.multiple_of((2 * x + l) * ROWS, ROWS), ROWS), :]
        theirs[x * ROWS:(x + 1) * ROWS, :] = total[pl.ds(pl.multiple_of((2 * x + 1 - l) * ROWS, ROWS), ROWS), :]


def right_kernel(mine, theirs, scales, right, message):
    own_half = mine[...] * scales[0:1, :]
    other_half = theirs[...] * scales[1:2, :]
    bound = jnp.sum(jnp.abs(own_half) + jnp.abs(other_half), axis=1, keepdims=True)
    power = exponent(0.125 * bound)
    factor = jnp.exp2(15.0 - power)
    high, low = split(own_half * factor)
    high2, low2 = split(other_half * factor)
    for lane in range(0, WIDTH, 512):
        near, far = right[0, :, lane:lane + 512], right[1, :, lane:lane + 512]
        message[:, lane:lane + 512] = (
            dot(high, near, (1, 0)) + dot(low, near, (1, 0)) + dot(high2, far, (1, 0)) + dot(low2, far, (1, 0))
        )
    message[:, WIDTH:] = jnp.broadcast_to(power, (4 * ROWS, LANES))


def moment_kernel(got, moment1, moment2, first_new, second_new, message):
    rotated = jnp.zeros((ROWS, WIDTH), F32)
    for source in range(4):
        rotated += got[source, :, :WIDTH] * jnp.exp2(got[source, :, WIDTH:WIDTH + 1] - 15.0)
    first = beta_one * moment1[...] + (1.0 - beta_one) * rotated
    second = beta_two * moment2[...] + (1.0 - beta_two) * rotated * rotated
    first_new[...] = first
    second_new[...] = second
    direction = first / corr_one / (jnp.sqrt(second / corr_two) + epsilon)
    power = exponent(jnp.max(jnp.abs(direction), axis=1, keepdims=True))
    message[:, :WIDTH] = direction * jnp.exp2(15.0 - power)
    message[:, WIDTH:] = jnp.broadcast_to(power, (ROWS, LANES))


def back_kernel(got, scales, right, mine, theirs):
    power = got[:, WIDTH:WIDTH + 1]
    high, low = split(got[:, :WIDTH])
    factor = jnp.exp2(power - 15.0)
    near, far = right[0, :, :WIDTH], right[1, :, :WIDTH]
    mine[...] = (dot(high, near, (1, 1)) + dot(low, near, (1, 1))) * factor * scales[0:1, :]
    theirs[:4 * ROWS, :] = (dot(high, far, (1, 1)) + dot(low, far, (1, 1))) * factor * scales[1:2, :]
    theirs[4 * ROWS:, :] = jnp.broadcast_to(jnp.max(power, axis=0, keepdims=True), (8, SLICE))


def update_kernel(place, factor, own, other, mine, theirs, update, parts):
    l = lax.rem(place[1], 2)
    for x in range(4):
        for values, side in ((mine, l), (theirs, 1 - l)):
            high, low = split(values[x * ROWS:(x + 1) * ROWS, :] * factor[0])
            rows = pl.ds(pl.multiple_of((2 * x + side) * ROWS, ROWS), ROWS)
            parts[rows, :SLICE] = high
            parts[rows, SLICE:] = low
    tiles = (own, other)
    values = [dot(tile[:, :PLANE], parts[...], (1, 0)) for tile in tiles]
    values = [value[:, :SLICE] + value[:, SLICE:] for value in values]
    for part, row, start in block_starts(place):
        scale = tiles[part][row:row + ROWS, PLANE:].astype(F32)
        for lane in range(0, SLICE, LANES):
            update[pl.ds(start, ROWS), lane:lane + LANES] = values[part][row:row + ROWS, lane:lane + LANES] * scale


def ring_gather(value, axes, names):
    size = len(names)
    blocks = [value]
    for shift in range(1, size):
        blocks.append(lax.ppermute(value, axes, [(names[i], names[(i + shift) % size]) for i in range(size)]))
    return jnp.concatenate(blocks)


def body(grad, left_codes, left_scale, right_codes, right_scale, moment1, moment2):
    zh, zl, x, l, h, c = (lax.axis_index(a) for a in AXES)
    place = jnp.stack([c, 2 * h + l, x]).astype(jnp.int32)
    right = with_lanes(right_codes, right_scale[..., None])
    right = jnp.concatenate([right, lax.ppermute(right, "l", SWAP)])

    pieces = with_lanes(left_codes, left_scale[..., None])
    first, second = left_perms()
    got1 = lax.ppermute(jnp.where(l == 0, pieces[0], pieces[1]), AXES, first)
    got2 = lax.ppermute(jnp.where(l == 0, pieces[1], pieces[0]), AXES, second)

    right, got1, got2 = lax.optimization_barrier((right, got1, got2))
    right = lax.all_gather(right, ("zh", "zl"), axis=1, tiled=True)
    slices = grad.reshape(ROWS, 8, 8, 32).transpose(2, 0, 1, 3).reshape(1, 8, ROWS, SLICE)
    columns = jnp.broadcast_to(slices, (4, 8, ROWS, SLICE)).reshape(32, ROWS, SLICE)
    columns = lax.all_to_all(columns, ("zl", "x", "l"), 0, 0, tiled=True).reshape(WIDTH, SLICE)

    chunk = jnp.where(zh == 0, jnp.concatenate([got1, got2]), jnp.concatenate([got2, got1]))
    left_own = ring_gather(ring_gather(chunk, ("x",), (0, 1, 2, 3)), ("l", "h"), (0, 2, 1, 3))
    left_other = lax.ppermute(left_own, "c", SWAP)

    mine, theirs = call(
        left_kernel,
        [(4 * ROWS, SLICE)] * 2,
        [pltpu.VMEM((WIDTH, 2 * SLICE), BF16), pltpu.VMEM((PLANE, SLICE), F32)],
        1,
        (place, left_own, left_other, columns),
    )
    theirs = lax.ppermute(theirs, "l", SWAP)
    scales = right[:, :, WIDTH].astype(F32)
    (message,) = call(
        right_kernel, [(4 * ROWS, WIDTH + LANES)], operands=(mine, theirs, scales, right)
    )
    got = lax.all_to_all(message.astype(F16).reshape(4, ROWS, -1), "x", 0, 0, tiled=True)
    first_new, second_new, message = call(
        moment_kernel,
        [(ROWS, WIDTH)] * 2 + [(ROWS, WIDTH + LANES)],
        operands=(got.astype(F32), moment1, moment2),
    )
    message = message.astype(F16)
    got = lax.all_to_all(jnp.broadcast_to(message, (4,) + message.shape), "x", 0, 0, tiled=True)
    mine, theirs = call(
        back_kernel,
        [(4 * ROWS, SLICE), (4 * ROWS + 8, SLICE)],
        operands=(got.astype(F32).reshape(4 * ROWS, -1), scales, right),
    )
    top = theirs[-1, 0]
    theirs = lax.ppermute(theirs, "l", SWAP)
    top = jnp.maximum(top, theirs[-1, 0])
    lane = jnp.full((8, LANES), top)
    tops = jnp.where(jnp.arange(4) == zl, top, 0.0)
    for shift in range(1, 4):
        other = lax.ppermute(lane, "zl", [(i, (i + shift) % 4) for i in range(4)])
        tops = tops + jnp.where(jnp.arange(4) == (zl - shift) % 4, other[0, 0], 0.0)
    (update,) = call(
        update_kernel,
        [(WIDTH, SLICE)],
        [pltpu.VMEM((PLANE, 2 * SLICE), BF16)],
        2,
        (place, jnp.exp2(-1.0 - top).reshape(1), left_own, left_other, mine, theirs),
    )
    got = lax.all_to_all(update.astype(F16).reshape(32, ROWS, SLICE), ("zl", "x", "l"), 0, 0, tiled=True)
    factors = jnp.exp2(tops + 1.0)[:, None, None, None]
    update = jnp.sum(got.reshape(4, 8, ROWS, SLICE).astype(F32) * factors, axis=0)
    update = update.reshape(8, ROWS, 8, 32).transpose(1, 2, 0, 3).reshape(ROWS, WIDTH)
    return update, first_new, second_new


def solution(mesh):
    fine = Mesh(mesh.devices.reshape(SIZES), AXES)
    fsdp, tp = ("zh", "zl", "x", "l"), ("h", "c")
    return jax.shard_map(
        body,
        mesh=fine,
        in_specs=(P(fsdp, tp), P(None, fsdp, tp), P(None, fsdp), P(tp, fsdp, None), P(tp, fsdp), P(fsdp, tp), P(fsdp, tp)),
        out_specs=(P(fsdp, tp), P(fsdp, tp), P(fsdp, tp)),
        check_vma=False,
    )
```

```python
import jax
import jax.numpy as jnp
from jax import lax
from jax.experimental import pallas as pl
from jax.experimental.pallas import tpu as pltpu
from jax.sharding import Mesh, PartitionSpec as P

beta_one = 0.9
beta_two = 0.999
corr_one = 1.0 - 0.9**10
corr_two = 1.0 - 0.999**10
epsilon = 1e-08

AXES = ("zh", "zl", "x", "l", "h", "c")
SIZES = (2, 4, 4, 2, 2, 2)
F32, BF16, F16 = jnp.float32, jnp.bfloat16, jnp.float16
WIDTH = 2048
SLICE = 256
PLANE = 512
ROWS = 64
LANES = 128
SWAP = [(0, 1), (1, 0)]


def linear(zh, zl, x, l, h, c):
    index = 0
    for size, value in zip(SIZES, (zh, zl, x, l, h, c)):
        index = index * size + value
    return index


def left_perms():
    first, second = [], []
    for z in range(8):
        for x in range(4):
            for l in range(2):
                for t in range(4):
                    src = linear(z // 4, z % 4, x, l, t // 2, t % 2)
                    for perm, b in ((first, l), (second, 1 - l)):
                        perm.append((src, linear(b, t, x, z % 2, z // 2 % 2, z // 4)))
    return first, second


def split(value):
    high = value.astype(BF16)
    return high, (value - high.astype(F32)).astype(BF16)


def exponent(bound):
    return jnp.ceil(jnp.log2(jnp.maximum(bound, 1e-30))) + 1.0


def dot(a, b, dims):
    return lax.dot_general(a, b, ((dims[:1], dims[1:]), ((), ())), preferred_element_type=F32)


def with_lanes(value, lane):
    return jnp.concatenate([value, jnp.broadcast_to(lane, lane.shape[:-1] + (LANES,)).astype(value.dtype)], -1)


def call(kernel, out, scratch=(), smem=0, operands=()):
    specs = [pl.BlockSpec(memory_space=pltpu.SMEM)] * smem
    specs += [pl.BlockSpec(memory_space=pltpu.VMEM)] * (len(operands) - smem)
    return pl.pallas_call(
        kernel,
        out_shape=tuple(jax.ShapeDtypeStruct(shape, F32) for shape in out),
        in_specs=specs,
        out_specs=tuple(pl.BlockSpec(memory_space=pltpu.VMEM) for _ in out),
        scratch_shapes=list(scratch),
        compiler_params=pltpu.CompilerParams(vmem_limit_bytes=28 * 1024 * 1024),
    )(*operands)


def block_starts(place):
    c, y, x = place[0], place[1], place[2]
    for part in range(2):
        core = c if part == 0 else 1 - c
        for s in range(4):
            for t in range(4):
                block = core * 16 + lax.rem(y - s + 4, 4) * 4 + lax.rem(x - t + 4, 4)
                yield part, (s * 4 + t) * ROWS, pl.multiple_of(block * ROWS, ROWS)


def left_kernel(place, own, other, columns, mine, theirs, scaled, total):
    tiles = (own, other)
    for part, row, start in block_starts(place):
        scale = tiles[part][row:row + ROWS, PLANE:].astype(F32)
        here = part * 1024 + row
        for lane in range(0, SLICE, LANES):
            value = columns[pl.ds(start, ROWS), lane:lane + LANES].astype(F32) * scale
            high, low = split(value)
            scaled[here:here + ROWS, lane:lane + LANES] = high
            scaled[here:here + ROWS, SLICE + lane:SLICE + lane + LANES] = low
    half = dot(own[:, :PLANE], scaled[:1024], (0, 0)) + dot(other[:, :PLANE], scaled[1024:], (0, 0))
    total[...] = half[:, :SLICE] + half[:, SLICE:]
    l = lax.rem(place[1], 2)
    for s in range(4):
        x = lax.rem(place[2] + s, 4)
        mine[s * ROWS:(s + 1) * ROWS, :] = total[pl.ds(pl.multiple_of((2 * x + l) * ROWS, ROWS), ROWS), :]
        theirs[s * ROWS:(s + 1) * ROWS, :] = total[pl.ds(pl.multiple_of((2 * x + 1 - l) * ROWS, ROWS), ROWS), :]


def right_kernel(mine, theirs, scales, right, message):
    own_half = mine[...] * scales[0:1, :]
    other_half = theirs[...] * scales[1:2, :]
    bound = jnp.sum(jnp.abs(own_half) + jnp.abs(other_half), axis=1, keepdims=True)
    power = exponent(0.125 * bound)
    factor = jnp.exp2(15.0 - power)
    high, low = split(own_half * factor)
    high2, low2 = split(other_half * factor)
    for lane in range(0, WIDTH, 512):
        near, far = right[0, :, lane:lane + 512], right[1, :, lane:lane + 512]
        message[:, lane:lane + 512] = (
            dot(high, near, (1, 0)) + dot(low, near, (1, 0)) + dot(high2, far, (1, 0)) + dot(low2, far, (1, 0))
        )
    message[:, WIDTH:] = jnp.broadcast_to(power, (4 * ROWS, LANES))


def moment_kernel(own, got1, got2, got3, moment1, moment2, first_new, second_new, message):
    rotated = own[:ROWS, :WIDTH] * jnp.exp2(own[:ROWS, WIDTH:WIDTH + 1] - 15.0)
    for got in (got1, got2, got3):
        rotated += got[:, :WIDTH] * jnp.exp2(got[:, WIDTH:WIDTH + 1] - 15.0)
    first = beta_one * moment1[...] + (1.0 - beta_one) * rotated
    second = beta_two * moment2[...] + (1.0 - beta_two) * rotated * rotated
    first_new[...] = first
    second_new[...] = second
    direction = first / corr_one / (jnp.sqrt(second / corr_two) + epsilon)
    power = exponent(jnp.max(jnp.abs(direction), axis=1, keepdims=True))
    message[:, :WIDTH] = direction * jnp.exp2(15.0 - power)
    message[:, WIDTH:] = jnp.broadcast_to(power, (ROWS, LANES))


def back_kernel(own, got1, got2, got3, scales, right, mine, theirs, top, high, low):
    near, far = right[0, :, :WIDTH], right[1, :, :WIDTH]
    best = jnp.zeros((1, 1), F32) - 200.0
    factors = []
    for s, got in enumerate((own, got1, got2, got3)):
        power = got[:, WIDTH:WIDTH + 1]
        best = jnp.maximum(best, jnp.max(power, axis=0, keepdims=True))
        factors.append(jnp.exp2(power - 15.0))
        high[s * ROWS:(s + 1) * ROWS, :], low[s * ROWS:(s + 1) * ROWS, :] = split(got[:, :WIDTH])
    factor = jnp.concatenate(factors)
    mine[...] = (dot(high[...], near, (1, 1)) + dot(low[...], near, (1, 1))) * factor * scales[0:1, :]
    theirs[:4 * ROWS, :] = (dot(high[...], far, (1, 1)) + dot(low[...], far, (1, 1))) * factor * scales[1:2, :]
    top[...] = jnp.broadcast_to(best, (8, SLICE))
    theirs[4 * ROWS:, :] = jnp.broadcast_to(best, (8, SLICE))


def update_kernel(place, own, other, mine, theirs, top, update, tops, parts):
    l = lax.rem(place[1], 2)
    best = jnp.maximum(top[...], theirs[4 * ROWS:, :])
    tops[...] = best
    factor = jnp.exp2(-1.0 - best[0:1, :])
    for s in range(4):
        x = lax.rem(place[2] - s + 4, 4)
        for values, side in ((mine, l), (theirs, 1 - l)):
            high, low = split(values[s * ROWS:(s + 1) * ROWS, :] * factor)
            rows = pl.ds(pl.multiple_of((2 * x + side) * ROWS, ROWS), ROWS)
            parts[rows, :SLICE] = high
            parts[rows, SLICE:] = low
    tiles = (own, other)
    values = [dot(tile[:, :PLANE], parts[...], (1, 0)) for tile in tiles]
    values = [value[:, :SLICE] + value[:, SLICE:] for value in values]
    for part, row, start in block_starts(place):
        scale = tiles[part][row:row + ROWS, PLANE:].astype(F32)
        for lane in range(0, SLICE, LANES):
            update[pl.ds(start, ROWS), lane:lane + LANES] = values[part][row:row + ROWS, lane:lane + LANES] * scale


def shifted(value, axis, shift):
    return lax.ppermute(value, axis, [(i, (i + shift) % 4) for i in range(4)])


def ring_gather(value, axes, names):
    size = len(names)
    blocks = [value]
    for shift in range(1, size):
        blocks.append(lax.ppermute(value, axes, [(names[i], names[(i + shift) % size]) for i in range(size)]))
    return jnp.concatenate(blocks)


def body(grad, left_codes, left_scale, right_codes, right_scale, moment1, moment2):
    zh, zl, x, l, h, c = (lax.axis_index(a) for a in AXES)
    place = jnp.stack([c, 2 * h + l, x]).astype(jnp.int32)
    right = with_lanes(right_codes, right_scale[..., None])
    right = jnp.concatenate([right, lax.ppermute(right, "l", SWAP)])

    pieces = with_lanes(left_codes, left_scale[..., None])
    first, second = left_perms()
    got1 = lax.ppermute(jnp.where(l == 0, pieces[0], pieces[1]), AXES, first)
    got2 = lax.ppermute(jnp.where(l == 0, pieces[1], pieces[0]), AXES, second)

    right, got1, got2 = lax.optimization_barrier((right, got1, got2))
    right = lax.all_gather(right, ("zh", "zl"), axis=1, tiled=True)
    slices = grad.reshape(ROWS, 8, 8, 32).transpose(2, 0, 1, 3).reshape(1, 8, ROWS, SLICE)
    columns = jnp.broadcast_to(slices, (4, 8, ROWS, SLICE)).reshape(32, ROWS, SLICE)
    columns = lax.all_to_all(columns, ("zl", "x", "l"), 0, 0, tiled=True).reshape(WIDTH, SLICE)

    chunk = jnp.where(zh == 0, jnp.concatenate([got1, got2]), jnp.concatenate([got2, got1]))
    left_own = ring_gather(ring_gather(chunk, ("x",), (0, 1, 2, 3)), ("l", "h"), (0, 2, 1, 3))
    left_other = lax.ppermute(left_own, "c", SWAP)

    mine, theirs = call(
        left_kernel,
        [(4 * ROWS, SLICE)] * 2,
        [pltpu.VMEM((WIDTH, 2 * SLICE), BF16), pltpu.VMEM((PLANE, SLICE), F32)],
        1,
        (place, left_own, left_other, columns),
    )
    theirs = lax.ppermute(theirs, "l", SWAP)
    scales = right[:, :, WIDTH].astype(F32)
    (message,) = call(
        right_kernel, [(4 * ROWS, WIDTH + LANES)], operands=(mine, theirs, scales, right)
    )
    got = [shifted(message[s * ROWS:(s + 1) * ROWS].astype(F16), "x", s).astype(F32) for s in range(1, 4)]
    first_new, second_new, message = call(
        moment_kernel,
        [(ROWS, WIDTH)] * 2 + [(ROWS, WIDTH + LANES)],
        operands=(message, *got, moment1, moment2),
    )
    narrow = message.astype(F16)
    got = [shifted(narrow, "x", s).astype(F32) for s in range(1, 4)]
    mine, theirs, top = call(
        back_kernel,
        [(4 * ROWS, SLICE), (4 * ROWS + 8, SLICE), (8, SLICE)],
        [pltpu.VMEM((4 * ROWS, WIDTH), BF16)] * 2,
        operands=(message, *got, scales, right),
    )
    theirs = lax.ppermute(theirs, "l", SWAP)
    update, top = call(
        update_kernel,
        [(WIDTH, SLICE), (8, SLICE)],
        [pltpu.VMEM((PLANE, 2 * SLICE), BF16)],
        1,
        (place, left_own, left_other, mine, theirs, top),
    )
    planes = jnp.arange(4)[:, None, None, None]
    tops = jnp.where(planes == zl, top[:1], 0.0)
    for s in range(1, 4):
        tops = tops + jnp.where(planes == (zl - s) % 4, shifted(top, "zl", s)[:1], 0.0)
    got = lax.all_to_all(update.astype(F16).reshape(32, ROWS, SLICE), ("zl", "x", "l"), 0, 0, tiled=True)
    update = jnp.sum(got.reshape(4, 8, ROWS, SLICE).astype(F32) * jnp.exp2(tops + 1.0), axis=0)
    update = update.reshape(8, ROWS, 8, 32).transpose(1, 2, 0, 3).reshape(ROWS, WIDTH)
    return update, first_new, second_new


def solution(mesh):
    fine = Mesh(mesh.devices.reshape(SIZES), AXES)
    fsdp, tp = ("zh", "zl", "x", "l"), ("h", "c")
    return jax.shard_map(
        body,
        mesh=fine,
        in_specs=(P(fsdp, tp), P(None, fsdp, tp), P(None, fsdp), P(tp, fsdp, None), P(tp, fsdp), P(fsdp, tp), P(fsdp, tp)),
        out_specs=(P(fsdp, tp), P(fsdp, tp), P(fsdp, tp)),
        check_vma=False,
    )
```

```python
import jax
import jax.numpy as jnp
from jax import lax
from jax.experimental import pallas as pl
from jax.experimental.pallas import tpu as pltpu
from jax.sharding import Mesh, PartitionSpec as P

beta_one = 0.9
beta_two = 0.999
corr_one = 1.0 - 0.9**10
corr_two = 1.0 - 0.999**10
epsilon = 1e-08

AXES = ("zh", "zl", "x", "l", "h", "c")
SIZES = (2, 4, 4, 2, 2, 2)
F32, BF16, F16 = jnp.float32, jnp.bfloat16, jnp.float16
WIDTH = 2048
SLICE = 256
PLANE = 512
ROWS = 64
LANES = 128
SWAP = [(0, 1), (1, 0)]


def linear(zh, zl, x, l, h, c):
    index = 0
    for size, value in zip(SIZES, (zh, zl, x, l, h, c)):
        index = index * size + value
    return index


def left_perms():
    first, second = [], []
    for z in range(8):
        for x in range(4):
            for l in range(2):
                for t in range(4):
                    src = linear(z // 4, z % 4, x, l, t // 2, t % 2)
                    for perm, b in ((first, l), (second, 1 - l)):
                        perm.append((src, linear(b, t, x, z % 2, z // 2 % 2, z // 4)))
    return first, second


def split(value):
    high = value.astype(BF16)
    return high, (value - high.astype(F32)).astype(BF16)


def exponent(bound):
    return jnp.ceil(jnp.log2(jnp.maximum(bound, 1e-30))) + 1.0


def dot(a, b, dims):
    return lax.dot_general(a, b, ((dims[:1], dims[1:]), ((), ())), preferred_element_type=F32)


def with_lanes(value, lane):
    return jnp.concatenate([value, jnp.broadcast_to(lane, lane.shape[:-1] + (LANES,)).astype(value.dtype)], -1)


def call(kernel, out, scratch=(), smem=0, operands=(), loose=0):
    specs = [pl.BlockSpec(memory_space=pltpu.SMEM)] * smem
    specs += [pl.BlockSpec(memory_space=pltpu.VMEM)] * (len(operands) - smem - loose)
    specs += [pl.BlockSpec(memory_space=pl.ANY)] * loose
    return pl.pallas_call(
        kernel,
        out_shape=tuple(jax.ShapeDtypeStruct(shape, BF16 if len(shape) == 3 else F32) for shape in out),
        in_specs=specs,
        out_specs=tuple(pl.BlockSpec(memory_space=pltpu.VMEM) for _ in out),
        scratch_shapes=list(scratch),
        compiler_params=pltpu.CompilerParams(vmem_limit_bytes=28 * 1024 * 1024),
    )(*operands)


def row_scales(right):
    return jnp.transpose(right[:, WIDTH:].astype(F32))[0:1, :]


def block_starts(place):
    c, y, x = place[0], place[1], place[2]
    for part in range(2):
        core = c if part == 0 else 1 - c
        for s in range(4):
            for t in range(4):
                block = core * 16 + lax.rem(y - s + 4, 4) * 4 + lax.rem(x - t + 4, 4)
                yield part, (s * 4 + t) * ROWS, pl.multiple_of(block * ROWS, ROWS)


def left_kernel(place, own, other, columns, mine, theirs, scaled, total):
    tiles = (own, other)
    for part, row, start in block_starts(place):
        scale = tiles[part][row:row + ROWS, PLANE:].astype(F32)
        here = part * 1024 + row
        for lane in range(0, SLICE, LANES):
            value = columns[pl.ds(start, ROWS), lane:lane + LANES].astype(F32) * scale
            high, low = split(value)
            scaled[here:here + ROWS, lane:lane + LANES] = high
            scaled[here:here + ROWS, SLICE + lane:SLICE + lane + LANES] = low
    half = dot(own[:, :PLANE], scaled[:1024], (0, 0)) + dot(other[:, :PLANE], scaled[1024:], (0, 0))
    total[...] = half[:, :SLICE] + half[:, SLICE:]
    l = lax.rem(place[1], 2)
    for s in range(4):
        x = lax.rem(place[2] + s, 4)
        mine[s * ROWS:(s + 1) * ROWS, :] = total[pl.ds(pl.multiple_of((2 * x + l) * ROWS, ROWS), ROWS), :]
        theirs[s * ROWS:(s + 1) * ROWS, :] = total[pl.ds(pl.multiple_of((2 * x + 1 - l) * ROWS, ROWS), ROWS), :]


def right_kernel(place, mine, theirs, here, back1, back2, back3, on1, on2, on3, far, message, right, sems):
    z = place[3]
    copies = []
    for index, (block, shift) in enumerate(zip((here, on1, on2, on3, far, back3, back2, back1), range(8))):
        rows = pl.ds(pl.multiple_of(lax.rem(z + shift, 8) * 32, 32), 32)
        copies.append(pltpu.make_async_copy(block, right.at[:, rows, :], sems.at[index]))
    for copy in copies:
        copy.start()
    for copy in copies:
        copy.wait()
    own_half = mine[...] * row_scales(right.at[0])
    other_half = theirs[...] * row_scales(right.at[1])
    bound = jnp.sum(jnp.abs(own_half) + jnp.abs(other_half), axis=1, keepdims=True)
    power = exponent(0.125 * bound)
    factor = jnp.exp2(15.0 - power)
    high, low = split(own_half * factor)
    high2, low2 = split(other_half * factor)
    for lane in range(0, WIDTH, 512):
        near, far = right[0, :, lane:lane + 512], right[1, :, lane:lane + 512]
        message[:, lane:lane + 512] = (
            dot(high, near, (1, 0)) + dot(low, near, (1, 0)) + dot(high2, far, (1, 0)) + dot(low2, far, (1, 0))
        )
    message[:, WIDTH:] = jnp.broadcast_to(power, (4 * ROWS, LANES))


def moment_kernel(own, got1, got2, got3, moment1, moment2, first_new, second_new, message):
    rotated = own[:ROWS, :WIDTH] * jnp.exp2(own[:ROWS, WIDTH:WIDTH + 1] - 15.0)
    for got in (got1, got2, got3):
        rotated += got[:, :WIDTH] * jnp.exp2(got[:, WIDTH:WIDTH + 1] - 15.0)
    first = beta_one * moment1[...] + (1.0 - beta_one) * rotated
    second = beta_two * moment2[...] + (1.0 - beta_two) * rotated * rotated
    first_new[...] = first
    second_new[...] = second
    direction = first / corr_one / (jnp.sqrt(second / corr_two) + epsilon)
    power = exponent(jnp.max(jnp.abs(direction), axis=1, keepdims=True))
    message[:, :WIDTH] = direction * jnp.exp2(15.0 - power)
    message[:, WIDTH:] = jnp.broadcast_to(power, (ROWS, LANES))


def back_kernel(own, got1, got2, got3, right, mine, theirs, top, high, low):
    near, far = right[0, :, :WIDTH], right[1, :, :WIDTH]
    best = jnp.zeros((1, 1), F32) - 200.0
    factors = []
    for s, got in enumerate((own, got1, got2, got3)):
        power = got[:, WIDTH:WIDTH + 1]
        best = jnp.maximum(best, jnp.max(power, axis=0, keepdims=True))
        factors.append(jnp.exp2(power - 15.0))
        high[s * ROWS:(s + 1) * ROWS, :], low[s * ROWS:(s + 1) * ROWS, :] = split(got[:, :WIDTH])
    factor = jnp.concatenate(factors)
    mine[...] = (dot(high[...], near, (1, 1)) + dot(low[...], near, (1, 1))) * factor * row_scales(right.at[0])
    theirs[:4 * ROWS, :] = (dot(high[...], far, (1, 1)) + dot(low[...], far, (1, 1))) * factor * row_scales(right.at[1])
    top[...] = jnp.broadcast_to(best, (8, SLICE))
    theirs[4 * ROWS:, :] = jnp.broadcast_to(best, (8, SLICE))


def update_kernel(place, own, other, mine, theirs, top, update, tops, parts):
    l = lax.rem(place[1], 2)
    best = jnp.maximum(top[...], theirs[4 * ROWS:, :])
    tops[...] = best
    factor = jnp.exp2(-1.0 - best[0:1, :])
    for s in range(4):
        x = lax.rem(place[2] - s + 4, 4)
        for values, side in ((mine, l), (theirs, 1 - l)):
            high, low = split(values[s * ROWS:(s + 1) * ROWS, :] * factor)
            rows = pl.ds(pl.multiple_of((2 * x + side) * ROWS, ROWS), ROWS)
            parts[rows, :SLICE] = high
            parts[rows, SLICE:] = low
    tiles = (own, other)
    values = [dot(tile[:, :PLANE], parts[...], (1, 0)) for tile in tiles]
    values = [value[:, :SLICE] + value[:, SLICE:] for value in values]
    for part, row, start in block_starts(place):
        scale = tiles[part][row:row + ROWS, PLANE:].astype(F32)
        for lane in range(0, SLICE, LANES):
            update[pl.ds(start, ROWS), lane:lane + LANES] = values[part][row:row + ROWS, lane:lane + LANES] * scale


def shifted(value, axis, shift):
    return lax.ppermute(value, axis, [(i, (i + shift) % 4) for i in range(4)])


def around(value, shift):
    return lax.ppermute(value, ("zh", "zl"), [(i, (i + shift) % 8) for i in range(8)])


def ring_gather(value, axes, names):
    size = len(names)
    blocks = [value]
    for shift in range(1, size):
        blocks.append(lax.ppermute(value, axes, [(names[i], names[(i + shift) % size]) for i in range(size)]))
    return jnp.concatenate(blocks)


def body(grad, left_codes, left_scale, right_codes, right_scale, moment1, moment2):
    zh, zl, x, l, h, c = (lax.axis_index(a) for a in AXES)
    place = jnp.stack([c, 2 * h + l, x, 4 * zh + zl]).astype(jnp.int32)
    right = with_lanes(right_codes, right_scale[..., None])
    right = jnp.concatenate([right, lax.ppermute(right, "l", SWAP)])

    pieces = with_lanes(left_codes, left_scale[..., None])
    first, second = left_perms()
    got1 = lax.ppermute(jnp.where(l == 0, pieces[0], pieces[1]), AXES, first)
    got2 = lax.ppermute(jnp.where(l == 0, pieces[1], pieces[0]), AXES, second)

    slices = grad.reshape(ROWS, 8, 8, 32).transpose(2, 0, 1, 3).reshape(1, 8, ROWS, SLICE)
    columns = jnp.broadcast_to(slices, (4, 8, ROWS, SLICE)).reshape(32, ROWS, SLICE)
    columns = lax.all_to_all(columns, ("zl", "x", "l"), 0, 0, tiled=True).reshape(WIDTH, SLICE)

    chunk = jnp.where(zh == 0, jnp.concatenate([got1, got2]), jnp.concatenate([got2, got1]))
    chunk = ring_gather(chunk, ("x",), (0, 1, 2, 3))
    back1, on1 = around(right, 1), around(right, 7)
    left_own = ring_gather(chunk, ("l", "h"), (0, 2, 1, 3))
    back2, on2 = around(back1, 1), around(on1, 7)
    back3, on3 = around(back2, 1), around(on2, 7)
    left_own, back3, on3 = lax.optimization_barrier((left_own, back3, on3))
    left_other = lax.ppermute(left_own, "c", SWAP)
    far = around(back3, 1)

    mine, theirs = call(
        left_kernel,
        [(4 * ROWS, SLICE)] * 2,
        [pltpu.VMEM((WIDTH, 2 * SLICE), BF16), pltpu.VMEM((PLANE, SLICE), F32)],
        1,
        (place, left_own, left_other, columns),
    )
    theirs = lax.ppermute(theirs, "l", SWAP)
    message, right = call(
        right_kernel,
        [(4 * ROWS, WIDTH + LANES), (2, SLICE, WIDTH + LANES)],
        [pltpu.SemaphoreType.DMA((8,))],
        1,
        (place, mine, theirs, right, back1, back2, back3, on1, on2, on3, far),
        8,
    )
    got = [shifted(message[s * ROWS:(s + 1) * ROWS].astype(F16), "x", s).astype(F32) for s in range(1, 4)]
    first_new, second_new, message = call(
        moment_kernel,
        [(ROWS, WIDTH)] * 2 + [(ROWS, WIDTH + LANES)],
        operands=(message, *got, moment1, moment2),
    )
    narrow = message.astype(F16)
    got = [shifted(narrow, "x", s).astype(F32) for s in range(1, 4)]
    mine, theirs, top = call(
        back_kernel,
        [(4 * ROWS, SLICE), (4 * ROWS + 8, SLICE), (8, SLICE)],
        [pltpu.VMEM((4 * ROWS, WIDTH), BF16)] * 2,
        operands=(message, *got, right),
    )
    theirs = lax.ppermute(theirs, "l", SWAP)
    update, top = call(
        update_kernel,
        [(WIDTH, SLICE), (8, SLICE)],
        [pltpu.VMEM((PLANE, 2 * SLICE), BF16)],
        1,
        (place, left_own, left_other, mine, theirs, top),
    )
    planes = jnp.arange(4)[:, None, None, None]
    tops = jnp.where(planes == zl, top[:1], 0.0)
    for s in range(1, 4):
        tops = tops + jnp.where(planes == (zl - s) % 4, shifted(top, "zl", s)[:1], 0.0)
    got = lax.all_to_all(update.astype(F16).reshape(32, ROWS, SLICE), ("zl", "x", "l"), 0, 0, tiled=True)
    update = jnp.sum(got.reshape(4, 8, ROWS, SLICE).astype(F32) * jnp.exp2(tops + 1.0), axis=0)
    update = update.reshape(8, ROWS, 8, 32).transpose(1, 2, 0, 3).reshape(ROWS, WIDTH)
    return update, first_new, second_new


def solution(mesh):
    fine = Mesh(mesh.devices.reshape(SIZES), AXES)
    fsdp, tp = ("zh", "zl", "x", "l"), ("h", "c")
    return jax.shard_map(
        body,
        mesh=fine,
        in_specs=(P(fsdp, tp), P(None, fsdp, tp), P(None, fsdp), P(tp, fsdp, None), P(tp, fsdp), P(fsdp, tp), P(fsdp, tp)),
        out_specs=(P(fsdp, tp), P(fsdp, tp), P(fsdp, tp)),
        check_vma=False,
    )
```

```python
import jax
import jax.numpy as jnp
from jax import lax
from jax.experimental import pallas as pl
from jax.experimental.pallas import tpu as pltpu
from jax.sharding import Mesh, PartitionSpec as P

beta_one = 0.9
beta_two = 0.999
corr_one = 1.0 - 0.9**10
corr_two = 1.0 - 0.999**10
epsilon = 1e-08

AXES = ("zh", "zl", "x", "l", "h", "c")
SIZES = (2, 4, 4, 2, 2, 2)
F32, BF16, F16 = jnp.float32, jnp.bfloat16, jnp.float16
WIDTH = 2048
SLICE = 256
PLANE = 512
ROWS = 64
LANES = 128
SWAP = [(0, 1), (1, 0)]


def linear(zh, zl, x, l, h, c):
    index = 0
    for size, value in zip(SIZES, (zh, zl, x, l, h, c)):
        index = index * size + value
    return index


def left_perms():
    first, second = [], []
    for z in range(8):
        for x in range(4):
            for l in range(2):
                for t in range(4):
                    src = linear(z // 4, z % 4, x, l, t // 2, t % 2)
                    for perm, b in ((first, l), (second, 1 - l)):
                        perm.append((src, linear(b, t, x, z % 2, z // 2 % 2, z // 4)))
    return first, second


def split(value):
    high = value.astype(BF16)
    return high, (value - high.astype(F32)).astype(BF16)


def exponent(bound):
    return jnp.ceil(jnp.log2(jnp.maximum(bound, 1e-30))) + 1.0


def dot(a, b, dims):
    return lax.dot_general(a, b, ((dims[:1], dims[1:]), ((), ())), preferred_element_type=F32)


def with_lanes(value, lane):
    return jnp.concatenate([value, jnp.broadcast_to(lane, lane.shape[:-1] + (LANES,)).astype(value.dtype)], -1)


def call(kernel, out, scratch=(), smem=0, operands=(), loose=0):
    specs = [pl.BlockSpec(memory_space=pltpu.SMEM)] * smem
    specs += [pl.BlockSpec(memory_space=pltpu.VMEM)] * (len(operands) - smem - loose)
    specs += [pl.BlockSpec(memory_space=pl.ANY)] * loose
    return pl.pallas_call(
        kernel,
        out_shape=tuple(jax.ShapeDtypeStruct(shape, BF16 if len(shape) == 3 else F32) for shape in out),
        in_specs=specs,
        out_specs=tuple(pl.BlockSpec(memory_space=pltpu.VMEM) for _ in out),
        scratch_shapes=list(scratch),
        compiler_params=pltpu.CompilerParams(vmem_limit_bytes=28 * 1024 * 1024),
    )(*operands)


def row_scales(right):
    return jnp.transpose(right[:, WIDTH:].astype(F32))[0:1, :]


def block_starts(place):
    c, y, x = place[0], place[1], place[2]
    for part in range(2):
        core = c if part == 0 else 1 - c
        for s in range(4):
            for t in range(4):
                block = core * 16 + lax.rem(y - s + 4, 4) * 4 + lax.rem(x - t + 4, 4)
                yield part, (s * 4 + t) * ROWS, pl.multiple_of(block * ROWS, ROWS)


def left_kernel(place, own, other, columns, mine, theirs, scaled, total):
    tiles = (own, other)
    for part, row, start in block_starts(place):
        scale = tiles[part][row:row + ROWS, PLANE:].astype(F32)
        here = part * 1024 + row
        for lane in range(0, SLICE, LANES):
            value = columns[pl.ds(start, ROWS), lane:lane + LANES].astype(F32) * scale
            high, low = split(value)
            scaled[here:here + ROWS, lane:lane + LANES] = high
            scaled[here:here + ROWS, SLICE + lane:SLICE + lane + LANES] = low
    half = dot(own[:, :PLANE], scaled[:1024], (0, 0)) + dot(other[:, :PLANE], scaled[1024:], (0, 0))
    total[...] = half[:, :SLICE] + half[:, SLICE:]
    l = lax.rem(place[1], 2)
    for s in range(4):
        x = lax.rem(place[2] + s, 4)
        mine[s * ROWS:(s + 1) * ROWS, :] = total[pl.ds(pl.multiple_of((2 * x + l) * ROWS, ROWS), ROWS), :]
        theirs[s * ROWS:(s + 1) * ROWS, :] = total[pl.ds(pl.multiple_of((2 * x + 1 - l) * ROWS, ROWS), ROWS), :]


def order_kernel(place, here, back1, back2, back3, on1, on2, on3, far, right, sems):
    z = place[3]
    copies = []
    for index, (block, shift) in enumerate(zip((here, on1, on2, on3, far, back3, back2, back1), range(8))):
        rows = pl.ds(pl.multiple_of(lax.rem(z + shift, 8) * 32, 32), 32)
        copies.append(pltpu.make_async_copy(block, right.at[:, rows, :], sems.at[index]))
    for copy in copies:
        copy.start()
    for copy in copies:
        copy.wait()


def right_kernel(mine, theirs, right, message):
    own_half = mine[...] * row_scales(right.at[0])
    other_half = theirs[...] * row_scales(right.at[1])
    bound = jnp.sum(jnp.abs(own_half) + jnp.abs(other_half), axis=1, keepdims=True)
    power = exponent(0.125 * bound)
    factor = jnp.exp2(15.0 - power)
    high, low = split(own_half * factor)
    high2, low2 = split(other_half * factor)
    for lane in range(0, WIDTH, 512):
        near, far = right[0, :, lane:lane + 512], right[1, :, lane:lane + 512]
        message[:, lane:lane + 512] = (
            dot(high, near, (1, 0)) + dot(low, near, (1, 0)) + dot(high2, far, (1, 0)) + dot(low2, far, (1, 0))
        )
    message[:, WIDTH:] = jnp.broadcast_to(power, (4 * ROWS, LANES))


def moment_kernel(own, got1, got2, got3, moment1, moment2, first_new, second_new, message):
    rotated = own[:ROWS, :WIDTH] * jnp.exp2(own[:ROWS, WIDTH:WIDTH + 1] - 15.0)
    for got in (got1, got2, got3):
        rotated += got[:, :WIDTH] * jnp.exp2(got[:, WIDTH:WIDTH + 1] - 15.0)
    first = beta_one * moment1[...] + (1.0 - beta_one) * rotated
    second = beta_two * moment2[...] + (1.0 - beta_two) * rotated * rotated
    first_new[...] = first
    second_new[...] = second
    direction = first / corr_one / (jnp.sqrt(second / corr_two) + epsilon)
    power = exponent(jnp.max(jnp.abs(direction), axis=1, keepdims=True))
    message[:, :WIDTH] = direction * jnp.exp2(15.0 - power)
    message[:, WIDTH:] = jnp.broadcast_to(power, (ROWS, LANES))


def back_kernel(own, got1, got2, got3, right, mine, theirs, top, high, low):
    near, far = right[0, :, :WIDTH], right[1, :, :WIDTH]
    best = jnp.zeros((1, 1), F32) - 200.0
    factors = []
    for s, got in enumerate((own, got1, got2, got3)):
        power = got[:, WIDTH:WIDTH + 1]
        best = jnp.maximum(best, jnp.max(power, axis=0, keepdims=True))
        factors.append(jnp.exp2(power - 15.0))
        high[s * ROWS:(s + 1) * ROWS, :], low[s * ROWS:(s + 1) * ROWS, :] = split(got[:, :WIDTH])
    factor = jnp.concatenate(factors)
    mine[...] = (dot(high[...], near, (1, 1)) + dot(low[...], near, (1, 1))) * factor * row_scales(right.at[0])
    theirs[:4 * ROWS, :] = (dot(high[...], far, (1, 1)) + dot(low[...], far, (1, 1))) * factor * row_scales(right.at[1])
    top[...] = jnp.broadcast_to(best, (8, SLICE))
    theirs[4 * ROWS:, :] = jnp.broadcast_to(best, (8, SLICE))


def update_kernel(place, own, other, mine, theirs, top, update, tops, parts):
    l = lax.rem(place[1], 2)
    best = jnp.maximum(top[...], theirs[4 * ROWS:, :])
    tops[...] = best
    factor = jnp.exp2(-1.0 - best[0:1, :])
    for s in range(4):
        x = lax.rem(place[2] - s + 4, 4)
        for values, side in ((mine, l), (theirs, 1 - l)):
            high, low = split(values[s * ROWS:(s + 1) * ROWS, :] * factor)
            rows = pl.ds(pl.multiple_of((2 * x + side) * ROWS, ROWS), ROWS)
            parts[rows, :SLICE] = high
            parts[rows, SLICE:] = low
    tiles = (own, other)
    values = [dot(tile[:, :PLANE], parts[...], (1, 0)) for tile in tiles]
    values = [value[:, :SLICE] + value[:, SLICE:] for value in values]
    for part, row, start in block_starts(place):
        scale = tiles[part][row:row + ROWS, PLANE:].astype(F32)
        for lane in range(0, SLICE, LANES):
            update[pl.ds(start, ROWS), lane:lane + LANES] = values[part][row:row + ROWS, lane:lane + LANES] * scale


def shifted(value, axis, shift):
    return lax.ppermute(value, axis, [(i, (i + shift) % 4) for i in range(4)])


def around(value, shift):
    return lax.ppermute(value, ("zh", "zl"), [(i, (i + shift) % 8) for i in range(8)])


def ring_gather(value, axes, names):
    size = len(names)
    blocks = [value]
    for shift in range(1, size):
        blocks.append(lax.ppermute(value, axes, [(names[i], names[(i + shift) % size]) for i in range(size)]))
    return jnp.concatenate(blocks)


def body(grad, left_codes, left_scale, right_codes, right_scale, moment1, moment2):
    zh, zl, x, l, h, c = (lax.axis_index(a) for a in AXES)
    place = jnp.stack([c, 2 * h + l, x, 4 * zh + zl]).astype(jnp.int32)
    right = with_lanes(right_codes, right_scale[..., None])
    right = jnp.concatenate([right, lax.ppermute(right, "l", SWAP)])

    pieces = with_lanes(left_codes, left_scale[..., None])
    first, second = left_perms()
    got1 = lax.ppermute(jnp.where(l == 0, pieces[0], pieces[1]), AXES, first)
    got2 = lax.ppermute(jnp.where(l == 0, pieces[1], pieces[0]), AXES, second)

    slices = grad.reshape(ROWS, 8, 8, 32).transpose(2, 0, 1, 3).reshape(1, 8, ROWS, SLICE)
    columns = jnp.broadcast_to(slices, (4, 8, ROWS, SLICE)).reshape(32, ROWS, SLICE)
    columns = lax.all_to_all(columns, ("zl", "x", "l"), 0, 0, tiled=True).reshape(WIDTH, SLICE)

    chunk = jnp.where(zh == 0, jnp.concatenate([got1, got2]), jnp.concatenate([got2, got1]))
    chunk = ring_gather(chunk, ("x",), (0, 1, 2, 3))
    back1, on1 = around(right, 1), around(right, 7)
    left_own = ring_gather(chunk, ("l", "h"), (0, 2, 1, 3))
    back2, on2 = around(back1, 1), around(on1, 7)
    back3, on3 = around(back2, 1), around(on2, 7)
    left_own, back3, on3 = lax.optimization_barrier((left_own, back3, on3))
    left_other = lax.ppermute(left_own, "c", SWAP)
    far = around(back3, 1)

    mine, theirs = call(
        left_kernel,
        [(4 * ROWS, SLICE)] * 2,
        [pltpu.VMEM((WIDTH, 2 * SLICE), BF16), pltpu.VMEM((PLANE, SLICE), F32)],
        1,
        (place, left_own, left_other, columns),
    )
    theirs = lax.ppermute(theirs, "l", SWAP)
    (right,) = call(
        order_kernel,
        [(2, SLICE, WIDTH + LANES)],
        [pltpu.SemaphoreType.DMA((8,))],
        1,
        (place, right, back1, back2, back3, on1, on2, on3, far),
        8,
    )
    (message,) = call(right_kernel, [(4 * ROWS, WIDTH + LANES)], operands=(mine, theirs, right))
    got = [shifted(message[s * ROWS:(s + 1) * ROWS].astype(F16), "x", s).astype(F32) for s in range(1, 4)]
    first_new, second_new, message = call(
        moment_kernel,
        [(ROWS, WIDTH)] * 2 + [(ROWS, WIDTH + LANES)],
        operands=(message, *got, moment1, moment2),
    )
    narrow = message.astype(F16)
    got = [shifted(narrow, "x", s).astype(F32) for s in range(1, 4)]
    mine, theirs, top = call(
        back_kernel,
        [(4 * ROWS, SLICE), (4 * ROWS + 8, SLICE), (8, SLICE)],
        [pltpu.VMEM((4 * ROWS, WIDTH), BF16)] * 2,
        operands=(message, *got, right),
    )
    theirs = lax.ppermute(theirs, "l", SWAP)
    update, top = call(
        update_kernel,
        [(WIDTH, SLICE), (8, SLICE)],
        [pltpu.VMEM((PLANE, 2 * SLICE), BF16)],
        1,
        (place, left_own, left_other, mine, theirs, top),
    )
    planes = jnp.arange(4)[:, None, None, None]
    tops = jnp.where(planes == zl, top[:1], 0.0)
    for s in range(1, 4):
        tops = tops + jnp.where(planes == (zl - s) % 4, shifted(top, "zl", s)[:1], 0.0)
    got = lax.all_to_all(update.astype(F16).reshape(32, ROWS, SLICE), ("zl", "x", "l"), 0, 0, tiled=True)
    update = jnp.sum(got.reshape(4, 8, ROWS, SLICE).astype(F32) * jnp.exp2(tops + 1.0), axis=0)
    update = update.reshape(8, ROWS, 8, 32).transpose(1, 2, 0, 3).reshape(ROWS, WIDTH)
    return update, first_new, second_new


def solution(mesh):
    fine = Mesh(mesh.devices.reshape(SIZES), AXES)
    fsdp, tp = ("zh", "zl", "x", "l"), ("h", "c")
    return jax.shard_map(
        body,
        mesh=fine,
        in_specs=(P(fsdp, tp), P(None, fsdp, tp), P(None, fsdp), P(tp, fsdp, None), P(tp, fsdp), P(fsdp, tp), P(fsdp, tp)),
        out_specs=(P(fsdp, tp), P(fsdp, tp), P(fsdp, tp)),
        check_vma=False,
    )
```

```python
import jax
import jax.numpy as jnp
from jax import lax
from jax.experimental import pallas as pl
from jax.experimental.pallas import tpu as pltpu
from jax.sharding import Mesh, PartitionSpec as P

beta_one = 0.9
beta_two = 0.999
corr_one = 1.0 - 0.9**10
corr_two = 1.0 - 0.999**10
epsilon = 1e-08

AXES = ("zh", "zl", "x", "l", "h", "c")
SIZES = (2, 4, 4, 2, 2, 2)
F32, BF16, F16 = jnp.float32, jnp.bfloat16, jnp.float16
WIDTH = 2048
SLICE = 256
PLANE = 512
ROWS = 64
LANES = 128
SWAP = [(0, 1), (1, 0)]


def linear(zh, zl, x, l, h, c):
    index = 0
    for size, value in zip(SIZES, (zh, zl, x, l, h, c)):
        index = index * size + value
    return index


def left_perms():
    first, second = [], []
    for z in range(8):
        for x in range(4):
            for l in range(2):
                for t in range(4):
                    src = linear(z // 4, z % 4, x, l, t // 2, t % 2)
                    for perm, b in ((first, l), (second, 1 - l)):
                        perm.append((src, linear(b, t, x, z % 2, z // 2 % 2, z // 4)))
    return first, second


def split(value):
    high = value.astype(BF16)
    return high, (value - high.astype(F32)).astype(BF16)


def exponent(bound):
    return jnp.ceil(jnp.log2(jnp.maximum(bound, 1e-30))) + 1.0


def dot(a, b, dims):
    return lax.dot_general(a, b, ((dims[:1], dims[1:]), ((), ())), preferred_element_type=F32)


def with_lanes(value, lane):
    return jnp.concatenate([value, jnp.broadcast_to(lane, lane.shape[:-1] + (LANES,)).astype(value.dtype)], -1)


def call(kernel, out, scratch=(), smem=0, operands=(), loose=0):
    specs = [pl.BlockSpec(memory_space=pltpu.SMEM)] * smem
    specs += [pl.BlockSpec(memory_space=pltpu.VMEM)] * (len(operands) - smem - loose)
    specs += [pl.BlockSpec(memory_space=pl.ANY)] * loose
    return pl.pallas_call(
        kernel,
        out_shape=tuple(jax.ShapeDtypeStruct(shape, BF16 if len(shape) == 3 else F32) for shape in out),
        in_specs=specs,
        out_specs=tuple(pl.BlockSpec(memory_space=pltpu.VMEM) for _ in out),
        scratch_shapes=list(scratch),
        compiler_params=pltpu.CompilerParams(vmem_limit_bytes=28 * 1024 * 1024),
    )(*operands)


def row_scales(right):
    return jnp.transpose(right[:, WIDTH:].astype(F32))[0:1, :]


def block_starts(place):
    c, y, x = place[0], place[1], place[2]
    for part in range(2):
        core = c if part == 0 else 1 - c
        for s in range(4):
            for t in range(4):
                block = core * 16 + lax.rem(y - s + 4, 4) * 4 + lax.rem(x - t + 4, 4)
                yield part, (s * 4 + t) * ROWS, pl.multiple_of(block * ROWS, ROWS)


def left_kernel(place, own, other, columns, mine, theirs, scaled, total):
    tiles = (own, other)
    for part, row, start in block_starts(place):
        scale = tiles[part][row:row + ROWS, PLANE:].astype(F32)
        here = part * 1024 + row
        for lane in range(0, SLICE, LANES):
            value = columns[pl.ds(start, ROWS), lane:lane + LANES].astype(F32) * scale
            high, low = split(value)
            scaled[here:here + ROWS, lane:lane + LANES] = high
            scaled[here:here + ROWS, SLICE + lane:SLICE + lane + LANES] = low
    half = dot(own[:, :PLANE], scaled[:1024], (0, 0)) + dot(other[:, :PLANE], scaled[1024:], (0, 0))
    total[...] = half[:, :SLICE] + half[:, SLICE:]
    l = lax.rem(place[1], 2)
    for s in range(4):
        x = lax.rem(place[2] + s, 4)
        mine[s * ROWS:(s + 1) * ROWS, :] = total[pl.ds(pl.multiple_of((2 * x + l) * ROWS, ROWS), ROWS), :]
        theirs[s * ROWS:(s + 1) * ROWS, :] = total[pl.ds(pl.multiple_of((2 * x + 1 - l) * ROWS, ROWS), ROWS), :]


def order_kernel(place, here, back1, back2, back3, on1, on2, on3, far, right, sems):
    z = place[3]
    copies = []
    for index, (block, shift) in enumerate(zip((here, on1, on2, on3, far, back3, back2, back1), range(8))):
        rows = pl.ds(pl.multiple_of(lax.rem(z + shift, 8) * 32, 32), 32)
        copies.append(pltpu.make_async_copy(block, right.at[:, rows, :], sems.at[index]))
    for copy in copies:
        copy.start()
    for copy in copies:
        copy.wait()


def right_kernel(mine, theirs, right, message):
    own_half = mine[...] * row_scales(right.at[0])
    other_half = theirs[...] * row_scales(right.at[1])
    bound = jnp.sum(jnp.abs(own_half) + jnp.abs(other_half), axis=1, keepdims=True)
    power = exponent(0.125 * bound)
    factor = jnp.exp2(15.0 - power)
    high, low = split(own_half * factor)
    high2, low2 = split(other_half * factor)
    for lane in range(0, WIDTH, 512):
        near, far = right[0, :, lane:lane + 512], right[1, :, lane:lane + 512]
        message[:, lane:lane + 512] = (
            dot(high, near, (1, 0)) + dot(low, near, (1, 0)) + dot(high2, far, (1, 0)) + dot(low2, far, (1, 0))
        )
    message[:, WIDTH:] = jnp.broadcast_to(power, (4 * ROWS, LANES))


def moment_kernel(own, got1, got2, got3, moment1, moment2, first_new, second_new, message):
    rotated = own[:ROWS, :WIDTH] * jnp.exp2(own[:ROWS, WIDTH:WIDTH + 1] - 15.0)
    for got in (got1, got2, got3):
        rotated += got[:, :WIDTH] * jnp.exp2(got[:, WIDTH:WIDTH + 1] - 15.0)
    first = beta_one * moment1[...] + (1.0 - beta_one) * rotated
    second = beta_two * moment2[...] + (1.0 - beta_two) * rotated * rotated
    first_new[...] = first
    second_new[...] = second
    direction = first / corr_one / (jnp.sqrt(second / corr_two) + epsilon)
    power = exponent(jnp.max(jnp.abs(direction), axis=1, keepdims=True))
    message[:, :WIDTH] = direction * jnp.exp2(15.0 - power)
    message[:, WIDTH:] = jnp.broadcast_to(power, (ROWS, LANES))


def back_kernel(own, got1, got2, got3, right, mine, theirs, top, high, low):
    near, far = right[0, :, :WIDTH], right[1, :, :WIDTH]
    best = jnp.zeros((1, 1), F32) - 200.0
    factors = []
    for s, got in enumerate((own, got1, got2, got3)):
        power = got[:, WIDTH:WIDTH + 1]
        best = jnp.maximum(best, jnp.max(power, axis=0, keepdims=True))
        factors.append(jnp.exp2(power - 15.0))
        high[s * ROWS:(s + 1) * ROWS, :], low[s * ROWS:(s + 1) * ROWS, :] = split(got[:, :WIDTH])
    factor = jnp.concatenate(factors)
    mine[...] = (dot(high[...], near, (1, 1)) + dot(low[...], near, (1, 1))) * factor * row_scales(right.at[0])
    theirs[:4 * ROWS, :] = (dot(high[...], far, (1, 1)) + dot(low[...], far, (1, 1))) * factor * row_scales(right.at[1])
    top[...] = jnp.broadcast_to(best, (8, SLICE))
    theirs[4 * ROWS:, :] = jnp.broadcast_to(best, (8, SLICE))


def update_kernel(place, own, other, mine, theirs, top, update, tops, parts):
    l = lax.rem(place[1], 2)
    best = jnp.maximum(top[...], theirs[4 * ROWS:, :])
    tops[...] = best
    factor = jnp.exp2(-1.0 - best[0:1, :])
    for s in range(4):
        x = lax.rem(place[2] - s + 4, 4)
        for values, side in ((mine, l), (theirs, 1 - l)):
            high, low = split(values[s * ROWS:(s + 1) * ROWS, :] * factor)
            rows = pl.ds(pl.multiple_of((2 * x + side) * ROWS, ROWS), ROWS)
            parts[rows, :SLICE] = high
            parts[rows, SLICE:] = low
    tiles = (own, other)
    values = [dot(tile[:, :PLANE], parts[...], (1, 0)) for tile in tiles]
    values = [value[:, :SLICE] + value[:, SLICE:] for value in values]
    for part, row, start in block_starts(place):
        scale = tiles[part][row:row + ROWS, PLANE:].astype(F32)
        for lane in range(0, SLICE, LANES):
            update[pl.ds(start, ROWS), lane:lane + LANES] = values[part][row:row + ROWS, lane:lane + LANES] * scale


def shifted(value, axis, shift):
    return lax.ppermute(value, axis, [(i, (i + shift) % 4) for i in range(4)])


def around(value, shift):
    return lax.ppermute(value, ("zh", "zl"), [(i, (i + shift) % 8) for i in range(8)])


def ring_gather(value, axes, names):
    size = len(names)
    blocks = [value]
    for shift in range(1, size):
        blocks.append(lax.ppermute(value, axes, [(names[i], names[(i + shift) % size]) for i in range(size)]))
    return jnp.concatenate(blocks)


def body(grad, left_codes, left_scale, right_codes, right_scale, moment1, moment2):
    zh, zl, x, l, h, c = (lax.axis_index(a) for a in AXES)
    place = jnp.stack([c, 2 * h + l, x, 4 * zh + zl]).astype(jnp.int32)
    right = with_lanes(right_codes, right_scale[..., None])
    right = jnp.concatenate([right, lax.ppermute(right, "l", SWAP)])

    pieces = with_lanes(left_codes, left_scale[..., None])
    first, second = left_perms()
    got1 = lax.ppermute(jnp.where(l == 0, pieces[0], pieces[1]), AXES, first)
    got2 = lax.ppermute(jnp.where(l == 0, pieces[1], pieces[0]), AXES, second)

    slices = grad.reshape(ROWS, 8, 8, 32).transpose(2, 0, 1, 3).reshape(1, 8, ROWS, SLICE)
    columns = jnp.broadcast_to(slices, (4, 8, ROWS, SLICE)).reshape(32, ROWS, SLICE)
    columns = lax.all_to_all(columns, ("zl", "x", "l"), 0, 0, tiled=True).reshape(WIDTH, SLICE)

    chunk = jnp.where(zh == 0, jnp.concatenate([got1, got2]), jnp.concatenate([got2, got1]))
    chunk = ring_gather(chunk, ("x",), (0, 1, 2, 3))
    back1, on1 = around(right, 1), around(right, 7)
    left_own = ring_gather(chunk, ("l", "h"), (0, 2, 1, 3))
    back2, on2 = around(back1, 1), around(on1, 7)
    back3, on3 = around(back2, 1), around(on2, 7)
    left_own, back3, on3 = lax.optimization_barrier((left_own, back3, on3))
    left_other = lax.ppermute(left_own, "c", SWAP)
    far = around(back3, 1)

    mine, theirs = call(
        left_kernel,
        [(4 * ROWS, SLICE)] * 2,
        [pltpu.VMEM((WIDTH, 2 * SLICE), BF16), pltpu.VMEM((PLANE, SLICE), F32)],
        1,
        (place, left_own, left_other, columns),
    )
    theirs = lax.ppermute(theirs, "l", SWAP)
    (right,) = call(
        order_kernel,
        [(2, SLICE, WIDTH + LANES)],
        [pltpu.SemaphoreType.DMA((8,))],
        1,
        (place, right, back1, back2, back3, on1, on2, on3, far),
        8,
    )
    (message,) = call(right_kernel, [(4 * ROWS, WIDTH + LANES)], operands=(mine, theirs, right))
    got = [shifted(message[s * ROWS:(s + 1) * ROWS].astype(F16), "x", s).astype(F32) for s in (2, 1, 3)]
    first_new, second_new, message = call(
        moment_kernel,
        [(ROWS, WIDTH)] * 2 + [(ROWS, WIDTH + LANES)],
        operands=(message, *got, moment1, moment2),
    )
    narrow = message.astype(F16)
    got = [shifted(narrow, "x", s).astype(F32) for s in (2, 1, 3)]
    got = [got[1], got[0], got[2]]
    mine, theirs, top = call(
        back_kernel,
        [(4 * ROWS, SLICE), (4 * ROWS + 8, SLICE), (8, SLICE)],
        [pltpu.VMEM((4 * ROWS, WIDTH), BF16)] * 2,
        operands=(message, *got, right),
    )
    theirs = lax.ppermute(theirs, "l", SWAP)
    update, top = call(
        update_kernel,
        [(WIDTH, SLICE), (8, SLICE)],
        [pltpu.VMEM((PLANE, 2 * SLICE), BF16)],
        1,
        (place, left_own, left_other, mine, theirs, top),
    )
    planes = jnp.arange(4)[:, None, None, None]
    tops = jnp.where(planes == zl, top[:1], 0.0)
    for s in range(1, 4):
        tops = tops + jnp.where(planes == (zl - s) % 4, shifted(top, "zl", s)[:1], 0.0)
    got = lax.all_to_all(update.astype(F16).reshape(32, ROWS, SLICE), ("zl", "x", "l"), 0, 0, tiled=True)
    update = jnp.sum(got.reshape(4, 8, ROWS, SLICE).astype(F32) * jnp.exp2(tops + 1.0), axis=0)
    update = update.reshape(8, ROWS, 8, 32).transpose(1, 2, 0, 3).reshape(ROWS, WIDTH)
    return update, first_new, second_new


def solution(mesh):
    fine = Mesh(mesh.devices.reshape(SIZES), AXES)
    fsdp, tp = ("zh", "zl", "x", "l"), ("h", "c")
    return jax.shard_map(
        body,
        mesh=fine,
        in_specs=(P(fsdp, tp), P(None, fsdp, tp), P(None, fsdp), P(tp, fsdp, None), P(tp, fsdp), P(fsdp, tp), P(fsdp, tp)),
        out_specs=(P(fsdp, tp), P(fsdp, tp), P(fsdp, tp)),
        check_vma=False,
    )
```
